256 devices in a mesh: dp: 64 (over z, x, core), expert: 4 (over y).
Axes of the slice: x: 4, y: 4, z: 8, core: 2. Of those that a mesh axis runs over, the one named last changes fastest.
Arguments:
- grads: bfloat16 [64, 1024, 3584], P('expert', 'dp'), may hold values from -60 to 60
- momentum: bfloat16 [64, 1024, 3584], P('expert', 'dp'), may hold values from -60 to 60
- owner: int32 [4, 16], P('expert'), may hold values from 0 to 15, each once within a row
- query_weight: bfloat16 [1536, 12288], P('dp'), may hold values from -6 to 6
- key_weight: bfloat16 [512, 8192], P('dp'), may hold values from -6 to 6
- head_maxima: float32 [256, 64], P(('dp', 'expert')), may hold values from 5 to 400
- clip_flags: int32 [64], replicated, may hold values 0 or 1
Outputs:
- new_momentum: bfloat16 [64, 1024, 3584], P('expert', 'dp')
- update: bfloat16 [64, 1024, 3584], P('expert', 'dp')
- owned_update: bfloat16 [4, 64, 1024, 896], P('expert', 'dp')
- clipped_query: bfloat16 [1536, 12288], P('dp')
- clipped_key: bfloat16 [512, 8192], P('dp')
The draws below stay inside these ranges and needn't reach their ends.
All inputs are finite; a program needn't handle non-finite values.
Results may differ from the reference program's by a relative error of at most 0.013.
Values may be sent and summed in bfloat16 or wider, within the bound.
A program may use at most 64 MiB of HBM per device.

```python
import math
import jax
import jax.numpy as jnp
from jax import lax

HID = 1024
DM = 3584
ITERS = 2
QRANK = 1536
KVRANK = 512
HEADS = 64
QNOPE = 128
QROPE = 64
MATS_GRP = 16
MATS = 64
LOGIT_ROWS = 256
N_DP = 64
N_EXPERT = 4


def shared_scales(key):
    row_key = jax.random.fold_in(key, 101)
    col_key = jax.random.fold_in(key, 102)
    row_scale = 10.0 ** jax.random.uniform(row_key, (MATS, HID, 1), jnp.float32)
    col_scale = 10.0 ** jax.random.uniform(col_key, (MATS, 1, DM), jnp.float32)
    return row_scale * col_scale / 8.0


def leading_part(key, ratio):
    row_key = jax.random.fold_in(key, 201)
    col_key = jax.random.fold_in(key, 202)
    weight_key = jax.random.fold_in(key, 203)
    row_factors = jnp.clip(jax.random.normal(row_key, (MATS, HID, 8), jnp.float32), -3.0, 3.0)
    col_factors = jnp.clip(jax.random.normal(col_key, (MATS, 8, DM), jnp.float32), -3.0, 3.0)
    term_weights = 0.9 * jax.random.uniform(weight_key, (MATS, 8), jnp.float32, minval=0.6, maxval=1.4)
    low_part = jnp.zeros((MATS, HID, DM), jnp.float32)
    for term in range(8):
        weight_now = term_weights[:, term] * ratio ** term
        low_part = low_part + weight_now[:, None, None] * row_factors[:, :, term][:, :, None] * col_factors[:, term, :][:, None, :]
    return low_part


def draw_grads(key, part):
    factor = shared_scales(key)
    key = jax.random.fold_in(key, 1)
    entries = jnp.clip(jax.random.normal(key, (MATS, HID, DM), jnp.float32), -4.0, 4.0)
    entries = entries + leading_part(key, 0.6)
    return jnp.clip(entries * factor, -60.0, 60.0).astype(jnp.bfloat16)


def draw_momentum(key, part):
    factor = shared_scales(key)
    key = jax.random.fold_in(key, 2)
    entries = jnp.clip(jax.random.normal(key, (MATS, HID, DM), jnp.float32), -4.0, 4.0)
    entries = entries + leading_part(key, 0.6)
    return jnp.clip(entries * factor, -60.0, 60.0).astype(jnp.bfloat16)


def draw_head_maxima(key, part):
    key = jax.random.fold_in(key, 3)
    row_key = jax.random.fold_in(key, 11)
    peak_key = jax.random.fold_in(key, 12)
    base_key = jax.random.fold_in(key, 13)
    peak_rows = jax.random.randint(row_key, (HEADS,), 0, LOGIT_ROWS)
    peak_values = 100.0 * 10.0 ** jax.random.uniform(peak_key, (HEADS,), jnp.float32, minval=-0.4, maxval=0.6)
    base_values = jax.random.uniform(base_key, (LOGIT_ROWS, HEADS), jnp.float32, minval=5.0, maxval=35.0)
    hits = jnp.arange(LOGIT_ROWS, dtype=jnp.int32)[:, None] == peak_rows[None, :]
    return jnp.where(hits, peak_values[None, :], base_values)


def plant(result, stream_key, least, high):
    longest = result.shape.index(max(result.shape))
    spots = []
    for shift in (0, 1):
        where = [jax.random.randint(jax.random.fold_in(stream_key, axis), (), 0, length) for axis, length in enumerate(result.shape)]
        where[longest] = (where[longest] + shift) % result.shape[longest]
        spots.append(tuple(where))
    return result.at[spots[0]].set(least).at[spots[1]].set(high)


def level_of(own_key, dims, split, low, largest):
    level, own = 1.0, jax.random.fold_in(own_key, 6)
    for position, parts in split:
        steps = jnp.exp(jax.random.uniform(jax.random.fold_in(own, position), (parts,), jnp.float32, low / len(split), largest / len(split)))
        level = level * jnp.repeat(steps, dims[position] // parts).reshape([-1 if axis == position else 1 for axis in range(len(dims))])
    return level


def normal_values(own_key, extent, scale, limit, pieces=(), kind=jnp.bfloat16):
    values = scale * jax.random.normal(own_key, extent, jnp.float32)
    if pieces:
        values = values * level_of(own_key, extent, pieces, -0.22, 0.18)
    return jnp.clip(values, -limit, limit).astype(kind)


def setup_inputs(seed: int = 0) -> dict:
    streams_of = jax.random.split(jax.random.key(seed), 8)
    grads = draw_grads(jax.random.fold_in(streams_of[7], 71), 0)
    momentum = draw_momentum(jax.random.fold_in(streams_of[7], 71), 0)
    owner = jax.vmap(lambda own: jax.random.permutation(own, MATS_GRP))(jax.random.split(streams_of[2], N_EXPERT)).reshape((N_EXPERT, MATS_GRP)).astype(jnp.int32)
    query_weight = normal_values(streams_of[3], (QRANK, HEADS * (QNOPE + QROPE)), 1.0, 6.0, ((0, 64),))
    key_weight = normal_values(streams_of[4], (KVRANK, HEADS * QNOPE), 1.0, 6.0, ((0, 64),))
    head_maxima = draw_head_maxima(jax.random.fold_in(streams_of[7], 71), 0)
    clip_flags = plant((jax.random.randint(streams_of[6], (HEADS,), 0, 4) < 3).astype(jnp.int32), jax.random.fold_in(streams_of[6], 1), 0, 1)
    return {"grads": grads, "momentum": momentum, "owner": owner, "query_weight": query_weight, "key_weight": key_weight, "head_maxima": head_maxima, "clip_flags": clip_flags}


MOMENTUM_DECAY = 0.95
COEF_A = 3.4445
COEF_B = -4.775
COEF_C = 2.0315
EPSILON = 1e-07
CLIP_TAU = 100.0

def orthogonal(matrix):
    squares = jnp.sum(jnp.square(matrix.astype(jnp.float32)))
    iterate = (matrix.astype(jnp.float32) * lax.rsqrt(squares + EPSILON)).astype(jnp.bfloat16)
    for sweep in range(ITERS):
        gram_sum = jnp.dot(iterate, iterate.T, preferred_element_type=jnp.float32).astype(jnp.bfloat16)
        poly_term = (COEF_B * gram_sum.astype(jnp.float32) + COEF_C * jnp.dot(gram_sum, gram_sum, preferred_element_type=jnp.float32)).astype(jnp.bfloat16)
        iterate = (COEF_A * iterate.astype(jnp.float32) + jnp.dot(poly_term, iterate, preferred_element_type=jnp.float32)).astype(jnp.bfloat16)
    return (iterate.astype(jnp.float32) * math.sqrt(DM)).astype(jnp.bfloat16)

def inverse_of(owners):
    group_ids = jnp.arange(owners.shape[0], dtype=jnp.int32)
    matches = owners[:, None] == group_ids[None, :]
    return lax.optimization_barrier(jnp.sum(jnp.where(matches, group_ids[:, None], 0), axis=0)).astype(jnp.int32)

def pick_rows(blocks_in, order_ids):
    return jnp.take(blocks_in, order_ids, axis=0)

def reference(grads, momentum, owner, query_weight, key_weight, head_maxima, clip_flags):
    new_momentum = (MOMENTUM_DECAY * momentum.astype(jnp.float32) + grads.astype(jnp.float32)).astype(jnp.bfloat16)
    update = lax.map(orthogonal, new_momentum)
    inverse = jax.vmap(inverse_of)(owner)
    grouped = update.reshape(N_EXPERT, MATS_GRP, HID, DM)
    owned = jax.vmap(pick_rows)(grouped, inverse)
    owned = owned.reshape(N_EXPERT, MATS_GRP, HID, 4, DM // 4).transpose(0, 1, 3, 2, 4)
    owned_update = owned.reshape(N_EXPERT, N_DP, HID, DM // 4)
    peak_values = lax.optimization_barrier(jnp.max(head_maxima, axis=0))
    clip_gamma = jnp.where(clip_flags == 1, jnp.minimum(1.0, CLIP_TAU / peak_values), 1.0)
    clip_root = jnp.sqrt(clip_gamma)
    query_heads = query_weight.astype(jnp.float32).reshape(QRANK, HEADS, QNOPE + QROPE)
    scaled = jnp.concatenate([query_heads[:, :, :QNOPE] * clip_root[None, :, None], query_heads[:, :, QNOPE:] * clip_gamma[None, :, None]], axis=2)
    clipped_query = scaled.reshape(QRANK, HEADS * (QNOPE + QROPE)).astype(jnp.bfloat16)
    key_heads = key_weight.astype(jnp.float32).reshape(KVRANK, HEADS, QNOPE) * clip_root[None, :, None]
    clipped_key = key_heads.reshape(KVRANK, HEADS * QNOPE).astype(jnp.bfloat16)
    return (new_momentum, update, owned_update, clipped_query, clipped_key)
```

```python
import functools
import math

import jax
import jax.numpy as jnp
from jax import lax
from jax.experimental import pallas as pl
from jax.experimental.pallas import tpu as pltpu
from jax.sharding import PartitionSpec as P

HEADS = 64
QNOPE = 128
QROPE = 64

MOMENTUM_DECAY = 0.95
COEF_A = 3.4445
COEF_B = -4.775
COEF_C = 2.0315
EPSILON = 1e-07
CLIP_TAU = 100.0

MESH = pl.DeviceIdType.MESH
PLANES = 8
SEATS = 8
ROWS = 16
MATS = 16
PLANE_ROWS = SEATS * ROWS
BLOCK = 2 * PLANE_ROWS
HID = PLANES * PLANE_ROWS
STEPS = HID // BLOCK
DEVICES = PLANES * SEATS
LANES = 128


def wrapped(value):
    return lax.rem(value + 64, 8)


def plane_offset(pair, half):
    return half + (1 - 2 * half) * pair * (pair + 1)


def dot_nn(a, b):
    return jnp.dot(a, b, preferred_element_type=jnp.float32)


def dot_nt(a, b):
    return lax.dot_general(a, b, (((1,), (1,)), ((), ())), preferred_element_type=jnp.float32)


def wait_bytes(ref, sem):
    pltpu.make_async_copy(ref, ref, sem).wait()


def step_kernel(
    experts,
    owner_s, grads_h, momentum_h, query_v, key_v, peaks_v, flags_v,
    new_momentum_h, returned_h, owned_h, query_o, key_o,
    grads_v, momentum_v, staged, new_v, x_own, x_pair, x_next, u_own,
    gram, poly, gram_next,
    part0, part1, part2, part3, far0, far1, far2, far3,
    peak_y, peak_z, peak_s, gamma_v, root_v,
    load_sem, store_sem, in_send, in_recv, pair_send, pair_recv,
    far_send, far_recv, share_send, share_recv, out_send, out_recv,
    peak_send, peak_recv,
):
    parts = (part0, part1, part2, part3)
    fars = (far0, far1, far2, far3)
    me = lax.axis_index("dp")
    y = lax.axis_index("expert")
    z = me // SEATS
    seat = lax.rem(me, SEATS)
    core = lax.rem(me, 2)
    group = me // 4
    width = grads_v.shape[2]
    quarter = width // 4
    pair = me + 1 - 2 * core
    across = me + 2 - 4 * lax.rem(me // 2, 2)

    def columns_of(part):
        return pl.ds(pl.multiple_of(part * quarter, LANES), quarter)

    my_columns = columns_of(lax.rem(me, 4))

    def remote(src, dst, send, recv, where):
        return pltpu.make_async_remote_copy(
            src_ref=src, dst_ref=dst, send_sem=send, recv_sem=recv,
            device_id=where, device_id_type=MESH,
        )

    barrier = pltpu.get_barrier_semaphore()

    def greet(i, carry):
        pl.semaphore_signal(
            barrier, inc=1, device_id={"dp": lax.rem(me + i, DEVICES)}, device_id_type=MESH
        )
        return carry

    lax.fori_loop(1, DEVICES, greet, 0)

    def greet_expert(i, carry):
        pl.semaphore_signal(
            barrier, inc=1, device_id={"expert": lax.rem(y + i, experts)}, device_id_type=MESH
        )
        return carry

    lax.fori_loop(1, experts, greet_expert, 0)

    load_grads = pltpu.make_async_copy(grads_h, grads_v, load_sem.at[0])
    load_momentum = pltpu.make_async_copy(momentum_h, momentum_v, load_sem.at[1])
    load_grads.start()
    load_momentum.start()
    peak_y[y] = jnp.zeros((8, LANES), jnp.float32)
    peak_y[y, :, 0:HEADS] = jnp.broadcast_to(peaks_v[...], (8, HEADS))
    load_grads.wait()
    load_momentum.wait()

    def momentum_of(k):
        return (
            MOMENTUM_DECAY * momentum_v[k].astype(jnp.float32) + grads_v[k].astype(jnp.float32)
        ).astype(jnp.bfloat16)

    def stage(g, carry):
        k = jnp.int32(0)
        for m in range(MATS):
            k = jnp.where(owner_s[0, m] == g, m, k)
        staged[g] = momentum_of(k)
        return carry

    lax.fori_loop(0, MATS, stage, 0)
    pl.semaphore_wait(barrier, DEVICES - 1 + experts - 1)

    def send_peak_y(i, carry):
        remote(
            peak_y.at[y], peak_y.at[y], peak_send.at[0], peak_recv.at[0],
            {"expert": lax.rem(y + i, experts)},
        ).start()
        return carry

    lax.fori_loop(1, experts, send_peak_y, 0)

    def send_rows(i, carry):
        t = i // SEATS
        step = lax.rem(t, STEPS)
        half = lax.rem(t // STEPS + z, 2)
        their_z = wrapped(z - plane_offset(step, half))
        their_seat = lax.rem(seat + lax.rem(i, SEATS), SEATS)
        there = their_z * SEATS + their_seat
        src = staged.at[there // 4, :, columns_of(lax.rem(there, 4))]
        row = (2 * step + half) * PLANE_ROWS + seat * ROWS
        dst = x_own.at[pl.ds(pl.multiple_of(row, ROWS), ROWS)]

        @pl.when(there != me)
        def _():
            remote(src, dst, in_send, in_recv.at[step], {"dp": there}).start()

        @pl.when(there == me)
        def _():
            pltpu.make_async_copy(src, dst, in_recv.at[step]).start()

        return carry

    lax.fori_loop(0, DEVICES, send_rows, 0)

    def new_momentum_step(k, carry):
        new_v[k] = momentum_of(k)
        return carry

    lax.fori_loop(0, MATS, new_momentum_step, 0)
    store_momentum = pltpu.make_async_copy(new_v, new_momentum_h, store_sem.at[0])
    store_momentum.start()

    wait_bytes(peak_y.at[pl.ds(0, experts - 1)], peak_recv.at[0])
    peak_z[z] = jnp.max(peak_y[...], axis=0)

    def send_peak_z(i, carry):
        remote(
            peak_z.at[z], peak_z.at[z], peak_send.at[1], peak_recv.at[1],
            {"dp": lax.rem(z + i, PLANES) * SEATS + seat},
        ).start()
        return carry

    lax.fori_loop(1, PLANES, send_peak_z, 0)

    def rows_of(s):
        return pl.ds(s * BLOCK, BLOCK)

    def mine_of(s, which):
        return pl.ds(pl.multiple_of(which * (s + 1) * LANES, LANES), (s + 1) * LANES)

    pair_copies = []
    far_copies = []
    share_copies = []

    def share(s):
        far_copies[s].wait_recv()
        spot = gram.at[rows_of(s), mine_of(s, core)]
        gram[rows_of(s), mine_of(s, core)] = (
            parts[s][...].astype(jnp.float32) + fars[s][...].astype(jnp.float32)
        ).astype(jnp.bfloat16)
        copy = remote(spot, spot, share_send.at[s], share_recv.at[s], {"dp": pair})
        copy.start()
        share_copies.append(copy)

    def mirror(s):
        share_copies[s].wait_recv()
        for j in range(s):
            gram[rows_of(j), rows_of(s)] = gram[rows_of(s), rows_of(j)].T

    for s in range(STEPS):
        wait_bytes(x_own.at[rows_of(s)], in_recv.at[s])
        copy = remote(
            x_own.at[rows_of(s)], x_pair.at[rows_of(s)], pair_send.at[s], pair_recv.at[s],
            {"dp": pair},
        )
        copy.start()
        pair_copies.append(copy)
        copy.wait_recv()
        parts[s][...] = (
            dot_nt(x_own[rows_of(s), :], x_own[mine_of(s, core), :])
            + dot_nt(x_pair[rows_of(s), :], x_pair[mine_of(s, core), :])
        ).astype(jnp.bfloat16)
        copy = remote(parts[s], fars[s], far_send.at[s], far_recv.at[s], {"dp": across})
        copy.start()
        far_copies.append(copy)
        if s > 0:
            share(s - 1)
        if s > 1:
            mirror(s - 2)
    mirror(STEPS - 2)
    share(STEPS - 1)
    mirror(STEPS - 1)

    diagonal = gram[rows_of(0), rows_of(0)].astype(jnp.float32)
    for s in range(1, STEPS):
        diagonal = diagonal + gram[rows_of(s), rows_of(s)].astype(jnp.float32)
    down = lax.broadcasted_iota(jnp.int32, (BLOCK, BLOCK), 0)
    along = lax.broadcasted_iota(jnp.int32, (BLOCK, BLOCK), 1)
    squares = jnp.sum(jnp.where(down == along, diagonal, 0.0), axis=0, keepdims=True)
    squares = jnp.sum(squares, axis=1, keepdims=True)
    scale = lax.rsqrt(squares + EPSILON)
    scale2 = 1.0 / (squares + EPSILON)

    def block_rows(i):
        return pl.ds(pl.multiple_of(i * BLOCK, BLOCK), BLOCK)

    def poly_step(i, carry):
        rows = block_rows(i)
        product = dot_nn(gram[rows, :], gram[...])
        poly[rows, :] = (
            (COEF_B * scale2) * gram[rows, :].astype(jnp.float32)
            + (COEF_C * scale2 * scale2) * product
        ).astype(jnp.bfloat16)
        return carry

    lax.fori_loop(0, STEPS, poly_step, 0)

    def iterate_step(i, carry):
        rows = block_rows(i)
        x_next[rows, :] = (
            scale
            * (COEF_A * x_own[rows, :].astype(jnp.float32) + dot_nn(poly[rows, :], x_own[...]))
        ).astype(jnp.bfloat16)
        return carry

    lax.fori_loop(0, STEPS, iterate_step, 0)

    def gram_step(i, carry):
        rows = block_rows(i)
        left = scale2 * (
            COEF_A * gram[rows, :].astype(jnp.float32) + dot_nn(poly[rows, :], gram[...])
        )
        gram_next[rows, :] = (
            COEF_A * left + dot_nn(left.astype(jnp.bfloat16), poly[...])
        ).astype(jnp.bfloat16)
        return carry

    lax.fori_loop(0, STEPS, gram_step, 0)

    wait_bytes(peak_z.at[pl.ds(0, PLANES - 1)], peak_recv.at[1])
    peak_s[seat] = jnp.max(peak_z[...], axis=0)

    def send_peak_s(i, carry):
        remote(
            peak_s.at[seat], peak_s.at[seat], peak_send.at[2], peak_recv.at[2],
            {"dp": z * SEATS + lax.rem(seat + i, SEATS)},
        ).start()
        return carry

    lax.fori_loop(1, SEATS, send_peak_s, 0)

    def update_step(i, carry):
        rows = block_rows(i)
        own = gram_next[rows, :]
        term = (
            COEF_B * own.astype(jnp.float32) + COEF_C * dot_nn(own, gram_next[...])
        ).astype(jnp.bfloat16)
        last = (
            COEF_A * x_next[rows, :].astype(jnp.float32) + dot_nn(term, x_next[...])
        ).astype(jnp.bfloat16)
        u_own[rows, :] = (last.astype(jnp.float32) * math.sqrt(width)).astype(jnp.bfloat16)

        def send_update(n, inner):
            half = n // SEATS
            their_z = wrapped(z + plane_offset(i, half))
            their_seat = lax.rem(seat + n, SEATS)
            there = their_z * SEATS + their_seat
            row = (2 * i + half) * PLANE_ROWS + their_seat * ROWS
            src = u_own.at[pl.ds(pl.multiple_of(row, ROWS), ROWS)]
            dst = returned_h.at[group, :, my_columns]

            @pl.when(there != me)
            def _():
                remote(src, dst, out_send, out_recv, {"dp": there}).start()

            @pl.when(there == me)
            def _():
                pltpu.make_async_copy(src, dst, out_recv).start()

            return inner

        lax.fori_loop(0, 2 * SEATS, send_update, 0)

        def store_owned(half, inner):
            src = u_own.at[pl.ds(pl.multiple_of((2 * i + half) * PLANE_ROWS, ROWS), PLANE_ROWS)]
            plane = wrapped(z + plane_offset(i, half))
            dst = owned_h.at[0, 0, pl.ds(pl.multiple_of(plane * PLANE_ROWS, ROWS), PLANE_ROWS)]
            pltpu.make_async_copy(src, dst, store_sem.at[1]).start()
            return inner

        lax.fori_loop(0, 2, store_owned, 0)
        return carry

    lax.fori_loop(0, STEPS, update_step, 0)

    wait_bytes(peak_s.at[pl.ds(0, SEATS - 1)], peak_recv.at[2])
    top = jnp.max(peak_s[...], axis=0)
    head_down = lax.broadcasted_iota(jnp.int32, (HEADS, HEADS), 0)
    head_along = lax.broadcasted_iota(jnp.int32, (HEADS, HEADS), 1)
    same = head_down == head_along
    peak = jnp.max(
        jnp.where(same, jnp.broadcast_to(top[0:1, 0:HEADS], (HEADS, HEADS)), 0.0),
        axis=1, keepdims=True,
    )
    flag = jnp.max(
        jnp.where(
            same, jnp.broadcast_to(flags_v[...].astype(jnp.float32), (HEADS, HEADS)), 0.0
        ),
        axis=1, keepdims=True,
    )
    peak = jnp.broadcast_to(peak, (HEADS, LANES))
    flag = jnp.broadcast_to(flag, (HEADS, LANES))
    gamma = jnp.where(flag == 1.0, jnp.minimum(1.0, CLIP_TAU / peak), 1.0)
    gamma_v[...] = gamma
    root_v[...] = jnp.sqrt(gamma)
    low = lax.broadcasted_iota(jnp.int32, (1, LANES), 1) < LANES // 2

    def clip_step(j, carry):
        root0 = root_v[pl.ds(2 * j, 1), :]
        root1 = root_v[pl.ds(2 * j + 1, 1), :]
        gamma0 = gamma_v[pl.ds(2 * j, 1), :]
        gamma1 = gamma_v[pl.ds(2 * j + 1, 1), :]
        scales = (root0, jnp.where(low, gamma0, root1), jnp.where(low, root1, gamma1))
        for n, factor in enumerate(scales):
            lanes = pl.ds(pl.multiple_of((3 * j + n) * LANES, LANES), LANES)
            query_o[:, lanes] = (query_v[:, lanes].astype(jnp.float32) * factor).astype(
                jnp.bfloat16
            )
        for n, factor in enumerate((root0, root1)):
            lanes = pl.ds(pl.multiple_of((2 * j + n) * LANES, LANES), LANES)
            key_o[:, lanes] = (key_v[:, lanes].astype(jnp.float32) * factor).astype(jnp.bfloat16)
        return carry

    lax.fori_loop(0, HEADS // 2, clip_step, 0)

    store_momentum.wait()
    wait_bytes(peak_y.at[pl.ds(0, experts - 1)], peak_send.at[0])
    wait_bytes(peak_z.at[pl.ds(0, PLANES - 1)], peak_send.at[1])
    wait_bytes(peak_s.at[pl.ds(0, SEATS - 1)], peak_send.at[2])
    for copy in pair_copies + far_copies + share_copies:
        copy.wait_send()
    wait_bytes(x_own.at[pl.ds(0, HID - ROWS)], in_send)
    wait_bytes(u_own.at[pl.ds(0, HID - ROWS)], out_send)
    wait_bytes(u_own, store_sem.at[1])
    wait_bytes(returned_h, out_recv)


def pick_kernel(owner_s, returned_h, update_h, sem):
    copies = [
        pltpu.make_async_copy(returned_h.at[owner_s[0, k]], update_h.at[k], sem.at[k])
        for k in range(MATS)
    ]
    for copy in copies:
        copy.start()
    for copy in copies:
        copy.wait()


def shards(experts, grads, momentum, owner, query_weight, key_weight, head_maxima, clip_flags):
    mats, rows, width = grads.shape
    quarter = width // 4
    smem = pl.BlockSpec(memory_space=pltpu.SMEM)
    vmem = pl.BlockSpec(memory_space=pltpu.VMEM)
    anywhere = pl.BlockSpec(memory_space=pl.ANY)
    bf16 = jnp.bfloat16
    shard = jax.ShapeDtypeStruct((mats, rows, width), bf16)
    block = pltpu.VMEM((mats, rows, width), bf16)
    half = pltpu.VMEM((HID, quarter), bf16)
    square = pltpu.VMEM((HID, HID), bf16)
    lanes = [pltpu.VMEM((BLOCK, (s + 1) * LANES), bf16) for s in range(STEPS)]
    dma = pltpu.SemaphoreType.DMA
    new_momentum, returned, owned, query, key = pl.pallas_call(
        functools.partial(step_kernel, experts),
        out_shape=(
            shard,
            shard,
            jax.ShapeDtypeStruct((1, 1, HID, quarter), bf16),
            jax.ShapeDtypeStruct(query_weight.shape, bf16),
            jax.ShapeDtypeStruct(key_weight.shape, bf16),
        ),
        in_specs=[smem, anywhere, anywhere, vmem, vmem, vmem, vmem],
        out_specs=(anywhere, anywhere, anywhere, vmem, vmem),
        scratch_shapes=[
            block, block, block, block, half, half, half, half, square, square, square,
            *lanes, *lanes,
            pltpu.VMEM((experts, 8, LANES), jnp.float32),
            pltpu.VMEM((PLANES, 8, LANES), jnp.float32),
            pltpu.VMEM((SEATS, 8, LANES), jnp.float32),
            pltpu.VMEM((HEADS, LANES), jnp.float32),
            pltpu.VMEM((HEADS, LANES), jnp.float32),
            dma((2,)), dma((2,)), dma, dma((STEPS,)), dma((STEPS,)), dma((STEPS,)),
            dma((STEPS,)), dma((STEPS,)), dma((STEPS,)), dma((STEPS,)), dma, dma,
            dma((3,)), dma((3,)),
        ],
        compiler_params=pltpu.CompilerParams(
            collective_id=0, has_side_effects=True, vmem_limit_bytes=48 * 1024 * 1024
        ),
        name="muon_step",
    )(
        owner, grads, momentum, query_weight, key_weight, head_maxima,
        clip_flags.reshape(1, HEADS),
    )
    update = pl.pallas_call(
        pick_kernel,
        out_shape=shard,
        in_specs=[smem, anywhere],
        out_specs=anywhere,
        scratch_shapes=[dma((MATS,))],
        name="pick_rows",
    )(owner, returned)
    return (new_momentum, update, owned, query, key)


def solution(mesh):
    in_specs = (
        P("expert", "dp", None),
        P("expert", "dp", None),
        P("expert", None),
        P("dp", None),
        P("dp", None),
        P(("dp", "expert"), None),
        P(),
    )
    out_specs = (
        P("expert", "dp", None),
        P("expert", "dp", None),
        P("expert", "dp", None, None),
        P("dp", None),
        P("dp", None),
    )
    return jax.shard_map(
        functools.partial(shards, mesh.shape["expert"]),
        mesh=mesh, in_specs=in_specs, out_specs=out_specs, check_vma=False,
    )
```

```python
import functools
import math

import jax
import jax.numpy as jnp
from jax import lax
from jax.experimental import pallas as pl
from jax.experimental.pallas import tpu as pltpu
from jax.sharding import PartitionSpec as P

HEADS = 64
QNOPE = 128
QROPE = 64

MOMENTUM_DECAY = 0.95
COEF_A = 3.4445
COEF_B = -4.775
COEF_C = 2.0315
EPSILON = 1e-07
CLIP_TAU = 100.0

MESH = pl.DeviceIdType.MESH
PLANES = 8
SEATS = 8
ROWS = 16
MATS = 16
PLANE_ROWS = SEATS * ROWS
BLOCK = 2 * PLANE_ROWS
HID = PLANES * PLANE_ROWS
DEVICES = PLANES * SEATS
LANES = 128

OFFSETS = (3, -3, 2, -2, 1, -1, 0, 4)
LOOK = 2
STEP_SLOTS = ((0, 1), (2, 3), (4, 5), (6,), (7,))
STEPS = len(STEP_SLOTS)
BLOCKS = HID // BLOCK


def wrapped(value):
    return lax.rem(value + 64, 8)


def step_extent(s):
    first = STEP_SLOTS[s][0] * PLANE_ROWS
    count = len(STEP_SLOTS[s]) * PLANE_ROWS
    return first, count, first + count


def part_shape(s):
    _, count, columns = step_extent(s)
    return (count, columns // 2) if columns % BLOCK == 0 and count == BLOCK else (count // 2, columns)


def dot_nn(a, b):
    return jnp.dot(a, b, preferred_element_type=jnp.float32)


def dot_nt(a, b):
    return lax.dot_general(a, b, (((1,), (1,)), ((), ())), preferred_element_type=jnp.float32)


def wait_bytes(ref, sem):
    pltpu.make_async_copy(ref, ref, sem).wait()


def step_kernel(
    experts,
    owner_h, grads_h, momentum_h, query_h, key_h, peaks_h, flags_h,
    new_momentum_h, returned_h, owned_h, query_out_h, key_out_h,
    owner_s, peaks_v, flags_v, query_v, key_v, query_o, key_o,
    grads_v, momentum_v, staged, new_v, x_own, x_pair, x_next, u_own,
    gram, poly, gram_next,
    part0, part1, part2, part3, part4, far0, far1, far2, far3, far4,
    peak_y, peak_z, peak_s, gamma_v, root_v,
    load_sem, store_sem, in_send, in_recv, pair_send, pair_recv,
    far_send, far_recv, share_send, share_recv, out_send, out_recv,
    peak_send, peak_recv,
):
    parts = (part0, part1, part2, part3, part4)
    fars = (far0, far1, far2, far3, far4)
    me = lax.axis_index("dp")
    y = lax.axis_index("expert")
    z = me // SEATS
    seat = lax.rem(me, SEATS)
    core = lax.rem(me, 2)
    group = me // 4
    width = grads_v.shape[2]
    quarter = width // 4
    pair = me + 1 - 2 * core
    across = me + 2 - 4 * lax.rem(me // 2, 2)

    def columns_of(part):
        return pl.ds(pl.multiple_of(part * quarter, LANES), quarter)

    my_columns = columns_of(lax.rem(me, 4))

    def remote(src, dst, send, recv, where):
        return pltpu.make_async_remote_copy(
            src_ref=src, dst_ref=dst, send_sem=send, recv_sem=recv,
            device_id=where, device_id_type=MESH,
        )

    loads = [
        pltpu.make_async_copy(src, dst, load_sem.at[n])
        for n, (src, dst) in enumerate(
            (
                (owner_h, owner_s),
                (grads_h, grads_v),
                (momentum_h, momentum_v),
                (peaks_h, peaks_v),
                (flags_h, flags_v),
                (query_h, query_v),
                (key_h, key_v),
            )
        )
    ]
    for load in loads:
        load.start()

    barrier = pltpu.get_barrier_semaphore()

    def greet(i, carry):
        pl.semaphore_signal(
            barrier, inc=1, device_id={"dp": lax.rem(me + i, DEVICES)}, device_id_type=MESH
        )
        return carry

    lax.fori_loop(1, DEVICES, greet, 0)

    def greet_expert(i, carry):
        pl.semaphore_signal(
            barrier, inc=1, device_id={"expert": lax.rem(y + i, experts)}, device_id_type=MESH
        )
        return carry

    lax.fori_loop(1, experts, greet_expert, 0)

    for load in loads[:4]:
        load.wait()
    peak_y[y] = jnp.zeros((8, LANES), jnp.float32)
    peak_y[y, :, 0:HEADS] = jnp.broadcast_to(peaks_v[...], (8, HEADS))

    def momentum_of(k):
        return (
            MOMENTUM_DECAY * momentum_v[k].astype(jnp.float32) + grads_v[k].astype(jnp.float32)
        ).astype(jnp.bfloat16)

    def stage(g, carry):
        k = jnp.int32(0)
        for m in range(MATS):
            k = jnp.where(owner_s[0, m] == g, m, k)
        staged[g] = momentum_of(k)
        return carry

    lax.fori_loop(0, MATS, stage, 0)
    pl.semaphore_wait(barrier, DEVICES - 1 + experts - 1)

    def send_peak_y(i, carry):
        remote(
            peak_y.at[y], peak_y.at[y], peak_send.at[0], peak_recv.at[0],
            {"expert": lax.rem(y + i, experts)},
        ).start()
        return carry

    lax.fori_loop(1, experts, send_peak_y, 0)

    def send_window(n):
        their_z = wrapped(z - OFFSETS[n])
        dst = x_own.at[pl.ds(pl.multiple_of(n * PLANE_ROWS + seat * ROWS, ROWS), ROWS)]
        arrival = in_recv.at[[n in slots for slots in STEP_SLOTS].index(True)]

        def send_rows(i, carry):
            there = their_z * SEATS + lax.rem(seat + i, SEATS)
            src = staged.at[there // 4, :, columns_of(lax.rem(there, 4))]

            @pl.when(there != me)
            def _():
                remote(src, dst, in_send.at[n], arrival, {"dp": there}).start()

            @pl.when(there == me)
            def _():
                pltpu.make_async_copy(src, dst, arrival).start()

            return carry

        lax.fori_loop(0, SEATS, send_rows, 0)

    def wait_window(n):
        sent = PLANE_ROWS - (ROWS if OFFSETS[n] == 0 else 0)
        wait_bytes(x_own.at[pl.ds(0, sent)], in_send.at[n])

    def send_next(first, last):
        for n in range(first, last):
            wait_window(n - LOOK)
            send_window(n)

    for n in range(LOOK):
        send_window(n)

    def new_momentum_step(k, carry):
        new_v[k] = momentum_of(k)
        return carry

    lax.fori_loop(0, MATS, new_momentum_step, 0)
    store_momentum = pltpu.make_async_copy(new_v, new_momentum_h, store_sem.at[0])
    store_momentum.start()

    wait_bytes(peak_y.at[pl.ds(0, experts - 1)], peak_recv.at[0])
    peak_z[z] = jnp.max(peak_y[...], axis=0)

    def send_peak_z(i, carry):
        remote(
            peak_z.at[z], peak_z.at[z], peak_send.at[1], peak_recv.at[1],
            {"dp": lax.rem(z + i, PLANES) * SEATS + seat},
        ).start()
        return carry

    lax.fori_loop(1, PLANES, send_peak_z, 0)

    def rows_of(i):
        return pl.ds(i * BLOCK, BLOCK)

    pair_copies = []
    far_copies = []
    share_copies = []

    def spot_of(s):
        first, count, columns = step_extent(s)
        rows, lanes = part_shape(s)
        if rows == count:
            return pl.ds(first, count), pl.ds(pl.multiple_of(core * lanes, LANES), lanes)
        return pl.ds(pl.multiple_of(first + core * rows, ROWS), rows), pl.ds(0, columns)

    def partial_gram(s):
        first, count, columns = step_extent(s)
        if part_shape(s)[0] == count:
            left, right = pl.ds(first, count), spot_of(s)[1]
        else:
            left, right = spot_of(s)[0], pl.ds(0, columns)
        return dot_nt(x_own[left, :], x_own[right, :]) + dot_nt(x_pair[left, :], x_pair[right, :])

    def share(s):
        far_copies[s].wait_recv()
        spot = spot_of(s)
        gram[spot] = (
            parts[s][...].astype(jnp.float32) + fars[s][...].astype(jnp.float32)
        ).astype(jnp.bfloat16)
        copy = remote(
            gram.at[spot], gram.at[spot], share_send.at[s], share_recv.at[s], {"dp": pair}
        )
        copy.start()
        share_copies.append(copy)

    def mirror(s):
        share_copies[s].wait_recv()
        first, count, _ = step_extent(s)
        if first:
            gram[0:first, first : first + count] = gram[first : first + count, 0:first].T

    for s in range(STEPS):
        send_next(
            min(PLANES, STEP_SLOTS[s][0] + LOOK), min(PLANES, STEP_SLOTS[s][-1] + 1 + LOOK)
        )
        first, count, _ = step_extent(s)
        arrived = pl.ds(first, count)
        wait_bytes(x_own.at[arrived], in_recv.at[s])
        copy = remote(
            x_own.at[arrived], x_pair.at[arrived], pair_send.at[s], pair_recv.at[s], {"dp": pair}
        )
        copy.start()
        pair_copies.append(copy)
        copy.wait_recv()
        parts[s][...] = partial_gram(s).astype(jnp.bfloat16)
        copy = remote(parts[s], fars[s], far_send.at[s], far_recv.at[s], {"dp": across})
        copy.start()
        far_copies.append(copy)
        if s > 0:
            share(s - 1)
        if s > 1:
            mirror(s - 2)
    mirror(STEPS - 2)
    share(STEPS - 1)
    mirror(STEPS - 1)

    diagonal = gram[rows_of(0), rows_of(0)].astype(jnp.float32)
    for i in range(1, BLOCKS):
        diagonal = diagonal + gram[rows_of(i), rows_of(i)].astype(jnp.float32)
    down = lax.broadcasted_iota(jnp.int32, (BLOCK, BLOCK), 0)
    along = lax.broadcasted_iota(jnp.int32, (BLOCK, BLOCK), 1)
    squares = jnp.sum(jnp.where(down == along, diagonal, 0.0), axis=0, keepdims=True)
    squares = jnp.sum(squares, axis=1, keepdims=True)
    scale = lax.rsqrt(squares + EPSILON)
    scale2 = 1.0 / (squares + EPSILON)

    for i in range(BLOCKS):
        rows = rows_of(i)
        poly[rows, :] = (
            (COEF_B * scale2) * gram[rows, :].astype(jnp.float32)
            + (COEF_C * scale2 * scale2) * dot_nn(gram[rows, :], gram[...])
        ).astype(jnp.bfloat16)

    for i in range(BLOCKS):
        rows = rows_of(i)
        x_next[rows, :] = (
            scale
            * (COEF_A * x_own[rows, :].astype(jnp.float32) + dot_nn(poly[rows, :], x_own[...]))
        ).astype(jnp.bfloat16)

    for i in range(BLOCKS):
        rows = rows_of(i)
        left = scale2 * (
            COEF_A * gram[rows, :].astype(jnp.float32) + dot_nn(poly[rows, :], gram[...])
        )
        gram_next[rows, :] = (
            COEF_A * left + dot_nn(left.astype(jnp.bfloat16), poly[...])
        ).astype(jnp.bfloat16)

    wait_bytes(peak_z.at[pl.ds(0, PLANES - 1)], peak_recv.at[1])
    peak_s[seat] = jnp.max(peak_z[...], axis=0)

    def send_peak_s(i, carry):
        remote(
            peak_s.at[seat], peak_s.at[seat], peak_send.at[2], peak_recv.at[2],
            {"dp": z * SEATS + lax.rem(seat + i, SEATS)},
        ).start()
        return carry

    lax.fori_loop(1, SEATS, send_peak_s, 0)

    def send_update(slot):
        plane = wrapped(z + OFFSETS[slot])
        first = slot * PLANE_ROWS

        def send_rows(i, carry):
            their_seat = lax.rem(seat + i, SEATS)
            there = plane * SEATS + their_seat
            src = u_own.at[pl.ds(pl.multiple_of(first + their_seat * ROWS, ROWS), ROWS)]
            dst = returned_h.at[group, :, my_columns]

            @pl.when(there != me)
            def _():
                remote(src, dst, out_send, out_recv, {"dp": there}).start()

            @pl.when(there == me)
            def _():
                pltpu.make_async_copy(src, dst, out_recv).start()

            return carry

        lax.fori_loop(0, SEATS, send_rows, 0)
        spot = owned_h.at[0, 0, pl.ds(pl.multiple_of(plane * PLANE_ROWS, ROWS), PLANE_ROWS)]
        pltpu.make_async_copy(
            u_own.at[pl.ds(first, PLANE_ROWS)], spot, store_sem.at[1]
        ).start()

    for i in range(BLOCKS):
        rows = rows_of(i)
        own = gram_next[rows, :]
        term = (
            COEF_B * own.astype(jnp.float32) + COEF_C * dot_nn(own, gram_next[...])
        ).astype(jnp.bfloat16)
        last = (
            COEF_A * x_next[rows, :].astype(jnp.float32) + dot_nn(term, x_next[...])
        ).astype(jnp.bfloat16)
        u_own[rows, :] = (last.astype(jnp.float32) * math.sqrt(width)).astype(jnp.bfloat16)
        send_update(2 * i)
        send_update(2 * i + 1)

    for load in loads[4:]:
        load.wait()
    wait_bytes(peak_s.at[pl.ds(0, SEATS - 1)], peak_recv.at[2])
    top = jnp.max(peak_s[...], axis=0)
    head_down = lax.broadcasted_iota(jnp.int32, (HEADS, HEADS), 0)
    head_along = lax.broadcasted_iota(jnp.int32, (HEADS, HEADS), 1)
    same = head_down == head_along
    peak = jnp.max(
        jnp.where(same, jnp.broadcast_to(top[0:1, 0:HEADS], (HEADS, HEADS)), 0.0),
        axis=1, keepdims=True,
    )
    flag = jnp.max(
        jnp.where(
            same, jnp.broadcast_to(flags_v[...].astype(jnp.float32), (HEADS, HEADS)), 0.0
        ),
        axis=1, keepdims=True,
    )
    peak = jnp.broadcast_to(peak, (HEADS, LANES))
    flag = jnp.broadcast_to(flag, (HEADS, LANES))
    gamma = jnp.where(flag == 1.0, jnp.minimum(1.0, CLIP_TAU / peak), 1.0)
    gamma_v[...] = gamma
    root_v[...] = jnp.sqrt(gamma)
    low = lax.broadcasted_iota(jnp.int32, (1, LANES), 1) < LANES // 2

    def clip_step(j, carry):
        root0 = root_v[pl.ds(2 * j, 1), :]
        root1 = root_v[pl.ds(2 * j + 1, 1), :]
        gamma0 = gamma_v[pl.ds(2 * j, 1), :]
        gamma1 = gamma_v[pl.ds(2 * j + 1, 1), :]
        scales = (root0, jnp.where(low, gamma0, root1), jnp.where(low, root1, gamma1))
        for n, factor in enumerate(scales):
            lanes = pl.ds(pl.multiple_of((3 * j + n) * LANES, LANES), LANES)
            query_o[:, lanes] = (query_v[:, lanes].astype(jnp.float32) * factor).astype(
                jnp.bfloat16
            )
        for n, factor in enumerate((root0, root1)):
            lanes = pl.ds(pl.multiple_of((2 * j + n) * LANES, LANES), LANES)
            key_o[:, lanes] = (key_v[:, lanes].astype(jnp.float32) * factor).astype(jnp.bfloat16)
        return carry

    lax.fori_loop(0, HEADS // 2, clip_step, 0)
    store_query = pltpu.make_async_copy(query_o, query_out_h, store_sem.at[2])
    store_key = pltpu.make_async_copy(key_o, key_out_h, store_sem.at[3])
    store_query.start()
    store_key.start()

    store_momentum.wait()
    store_query.wait()
    store_key.wait()
    wait_bytes(peak_y.at[pl.ds(0, experts - 1)], peak_send.at[0])
    wait_bytes(peak_z.at[pl.ds(0, PLANES - 1)], peak_send.at[1])
    wait_bytes(peak_s.at[pl.ds(0, SEATS - 1)], peak_send.at[2])
    for copy in pair_copies + far_copies + share_copies:
        copy.wait_send()
    for n in range(PLANES - LOOK, PLANES):
        wait_window(n)
    wait_bytes(u_own.at[pl.ds(0, HID - ROWS)], out_send)
    wait_bytes(u_own, store_sem.at[1])

    wait_bytes(returned_h, out_recv)


def finish_kernel(
    owner_h, new_momentum_i, returned_i, owned_i, query_i, key_i,
    new_momentum_h, update_h, owned_h, query_h, key_h,
    owner_s, new_momentum_v, update_v, owned_v, query_v, key_v,
    owner_sem, load_sem, store_sem, pick_sem, put_sem,
):
    load_owner = pltpu.make_async_copy(owner_h, owner_s, owner_sem)
    load_owner.start()
    plain = (
        (new_momentum_i, new_momentum_v, new_momentum_h),
        (owned_i, owned_v, owned_h),
        (query_i, query_v, query_h),
        (key_i, key_v, key_h),
    )
    loads = [
        pltpu.make_async_copy(src, mid, load_sem.at[n]) for n, (src, mid, _) in enumerate(plain)
    ]
    stores = [
        pltpu.make_async_copy(mid, dst, store_sem.at[n]) for n, (_, mid, dst) in enumerate(plain)
    ]
    for load in loads:
        load.start()
    load_owner.wait()
    picks = [
        pltpu.make_async_copy(returned_i.at[owner_s[0, k]], update_v.at[k], pick_sem.at[k])
        for k in range(MATS)
    ]
    puts = [
        pltpu.make_async_copy(update_v.at[k], update_h.at[k], put_sem.at[k]) for k in range(MATS)
    ]
    for pick in picks:
        pick.start()
    for load, store in zip(loads, stores):
        load.wait()
        store.start()
    for pick, put in zip(picks, puts):
        pick.wait()
        put.start()
    for copy in stores + puts:
        copy.wait()


def shards(experts, grads, momentum, owner, query_weight, key_weight, head_maxima, clip_flags):
    mats, rows, width = grads.shape
    quarter = width // 4
    anywhere = pl.BlockSpec(memory_space=pl.ANY)
    bf16 = jnp.bfloat16
    shard = jax.ShapeDtypeStruct((mats, rows, width), bf16)
    block = pltpu.VMEM((mats, rows, width), bf16)
    half = pltpu.VMEM((HID, quarter), bf16)
    square = pltpu.VMEM((HID, HID), bf16)
    lanes = [pltpu.VMEM(part_shape(s), bf16) for s in range(STEPS)]
    dma = pltpu.SemaphoreType.DMA
    results = (
        shard,
        shard,
        jax.ShapeDtypeStruct((1, 1, HID, quarter), bf16),
        jax.ShapeDtypeStruct(query_weight.shape, bf16),
        jax.ShapeDtypeStruct(key_weight.shape, bf16),
    )
    parts = pl.pallas_call(
        functools.partial(step_kernel, experts),
        out_shape=results,
        in_specs=[anywhere] * 7,
        out_specs=(anywhere,) * 5,
        scratch_shapes=[
            pltpu.SMEM((1, mats), jnp.int32),
            pltpu.VMEM((1, HEADS), jnp.float32),
            pltpu.VMEM((1, HEADS), jnp.int32),
            pltpu.VMEM(query_weight.shape, bf16),
            pltpu.VMEM(key_weight.shape, bf16),
            pltpu.VMEM(query_weight.shape, bf16),
            pltpu.VMEM(key_weight.shape, bf16),
            block, block, block, block, half, half, half, half, square, square, square,
            *lanes, *lanes,
            pltpu.VMEM((experts, 8, LANES), jnp.float32),
            pltpu.VMEM((PLANES, 8, LANES), jnp.float32),
            pltpu.VMEM((SEATS, 8, LANES), jnp.float32),
            pltpu.VMEM((HEADS, LANES), jnp.float32),
            pltpu.VMEM((HEADS, LANES), jnp.float32),
            dma((7,)), dma((4,)), dma((PLANES,)), dma((STEPS,)), dma((STEPS,)), dma((STEPS,)),
            dma((STEPS,)), dma((STEPS,)), dma((STEPS,)), dma((STEPS,)), dma, dma,
            dma((3,)), dma((3,)),
        ],
        compiler_params=pltpu.CompilerParams(
            collective_id=0, has_side_effects=True, vmem_limit_bytes=60 * 1024 * 1024
        ),
        name="muon_step",
    )(
        owner, grads, momentum, query_weight, key_weight, head_maxima,
        clip_flags.reshape(1, HEADS),
    )
    return pl.pallas_call(
        finish_kernel,
        out_shape=results,
        in_specs=[anywhere] * 6,
        out_specs=(anywhere,) * 5,
        scratch_shapes=[
            pltpu.SMEM((1, mats), jnp.int32),
            *[pltpu.VMEM(result.shape, bf16) for result in results],
            dma, dma((4,)), dma((4,)), dma((MATS,)), dma((MATS,)),
        ],
        compiler_params=pltpu.CompilerParams(vmem_limit_bytes=60 * 1024 * 1024),
        name="finish",
    )(owner, *parts)


def solution(mesh):
    in_specs = (
        P("expert", "dp", None),
        P("expert", "dp", None),
        P("expert", None),
        P("dp", None),
        P("dp", None),
        P(("dp", "expert"), None),
        P(),
    )
    out_specs = (
        P("expert", "dp", None),
        P("expert", "dp", None),
        P("expert", "dp", None, None),
        P("dp", None),
        P("dp", None),
    )
    return jax.shard_map(
        functools.partial(shards, mesh.shape["expert"]),
        mesh=mesh, in_specs=in_specs, out_specs=out_specs, check_vma=False,
    )
```

```python
import functools
import math

import jax
import jax.numpy as jnp
from jax import lax
from jax.experimental import pallas as pl
from jax.experimental.pallas import tpu as pltpu
from jax.sharding import PartitionSpec as P

HEADS = 64
QNOPE = 128
QROPE = 64

MOMENTUM_DECAY = 0.95
COEF_A = 3.4445
COEF_B = -4.775
COEF_C = 2.0315
EPSILON = 1e-07
CLIP_TAU = 100.0

MESH = pl.DeviceIdType.MESH
PLANES = 8
SEATS = 8
ROWS = 16
MATS = 16
PLANE_ROWS = SEATS * ROWS
BLOCK = 2 * PLANE_ROWS
HID = PLANES * PLANE_ROWS
DEVICES = PLANES * SEATS
LANES = 128

OFFSETS = (3, -3, 2, -2, 1, -1, 0, 4)
LOOK = 8
STEP_SLOTS = ((0, 1), (2, 3), (4, 5), (6,), (7,))
STEPS = len(STEP_SLOTS)
BLOCKS = HID // BLOCK


def wrapped(value):
    return lax.rem(value + 64, 8)


def step_extent(s):
    first = STEP_SLOTS[s][0] * PLANE_ROWS
    count = len(STEP_SLOTS[s]) * PLANE_ROWS
    return first, count, first + count


def part_shape(s):
    _, count, columns = step_extent(s)
    return (count, columns // 2) if columns % BLOCK == 0 and count == BLOCK else (count // 2, columns)


def dot_nn(a, b):
    return jnp.dot(a, b, preferred_element_type=jnp.float32)


def dot_nt(a, b):
    return lax.dot_general(a, b, (((1,), (1,)), ((), ())), preferred_element_type=jnp.float32)


def wait_bytes(ref, sem):
    pltpu.make_async_copy(ref, ref, sem).wait()


def step_kernel(
    experts,
    owner_h, grads_h, momentum_h, query_h, key_h, peaks_h, flags_h,
    new_momentum_h, returned_h, owned_h, query_out_h, key_out_h,
    owner_s, peaks_v, flags_v, query_v, key_v, query_o, key_o,
    grads_v, momentum_v, staged, new_v, x_own, x_pair, x_next, u_own,
    gram, poly, gram_next, left_v,
    part0, part1, part2, part3, part4, far0, far1, far2, far3, far4,
    peak_y, peak_z, peak_s, gamma_v, root_v,
    load_sem, store_sem, in_send, in_recv, pair_send, pair_recv,
    far_send, far_recv, share_send, share_recv, poly_send, poly_recv, next_send, next_recv,
    out_send, out_recv,
    peak_send, peak_recv,
):
    parts = (part0, part1, part2, part3, part4)
    fars = (far0, far1, far2, far3, far4)
    me = lax.axis_index("dp")
    y = lax.axis_index("expert")
    z = me // SEATS
    seat = lax.rem(me, SEATS)
    core = lax.rem(me, 2)
    group = me // 4
    width = grads_v.shape[2]
    quarter = width // 4
    pair = me + 1 - 2 * core
    across = me + 2 - 4 * lax.rem(me // 2, 2)

    def columns_of(part):
        return pl.ds(pl.multiple_of(part * quarter, LANES), quarter)

    my_columns = columns_of(lax.rem(me, 4))

    def remote(src, dst, send, recv, where):
        return pltpu.make_async_remote_copy(
            src_ref=src, dst_ref=dst, send_sem=send, recv_sem=recv,
            device_id=where, device_id_type=MESH,
        )

    loads = [
        pltpu.make_async_copy(src, dst, load_sem.at[n])
        for n, (src, dst) in enumerate(
            (
                (owner_h, owner_s),
                (grads_h, grads_v),
                (momentum_h, momentum_v),
                (peaks_h, peaks_v),
                (flags_h, flags_v),
                (query_h, query_v),
                (key_h, key_v),
            )
        )
    ]
    for load in loads:
        load.start()

    barrier = pltpu.get_barrier_semaphore()

    def greet(i, carry):
        pl.semaphore_signal(
            barrier, inc=1, device_id={"dp": lax.rem(me + i, DEVICES)}, device_id_type=MESH
        )
        return carry

    lax.fori_loop(1, DEVICES, greet, 0)

    def greet_expert(i, carry):
        pl.semaphore_signal(
            barrier, inc=1, device_id={"expert": lax.rem(y + i, experts)}, device_id_type=MESH
        )
        return carry

    lax.fori_loop(1, experts, greet_expert, 0)

    for load in loads[:4]:
        load.wait()
    peak_y[y] = jnp.zeros((8, LANES), jnp.float32)
    peak_y[y, :, 0:HEADS] = jnp.broadcast_to(peaks_v[...], (8, HEADS))

    def momentum_of(k):
        return (
            MOMENTUM_DECAY * momentum_v[k].astype(jnp.float32) + grads_v[k].astype(jnp.float32)
        ).astype(jnp.bfloat16)

    def stage(g, carry):
        k = jnp.int32(0)
        for m in range(MATS):
            k = jnp.where(owner_s[0, m] == g, m, k)
        staged[g] = momentum_of(k)
        return carry

    pl.semaphore_wait(barrier, DEVICES - 1 + experts - 1)

    def send_peak_y(i, carry):
        remote(
            peak_y.at[y], peak_y.at[y], peak_send.at[0], peak_recv.at[0],
            {"expert": lax.rem(y + i, experts)},
        ).start()
        return carry

    lax.fori_loop(1, experts, send_peak_y, 0)

    def send_window(n):
        their_z = wrapped(z - OFFSETS[n])
        lax.fori_loop(2 * their_z, 2 * their_z + 2, stage, 0)
        dst = x_own.at[pl.ds(pl.multiple_of(n * PLANE_ROWS + seat * ROWS, ROWS), ROWS)]
        arrival = in_recv.at[[n in slots for slots in STEP_SLOTS].index(True)]

        def send_rows(i, carry):
            there = their_z * SEATS + lax.rem(seat + i, SEATS)
            src = staged.at[there // 4, :, columns_of(lax.rem(there, 4))]

            @pl.when(there != me)
            def _():
                remote(src, dst, in_send.at[n], arrival, {"dp": there}).start()

            @pl.when(there == me)
            def _():
                pltpu.make_async_copy(src, dst, arrival).start()

            return carry

        lax.fori_loop(0, SEATS, send_rows, 0)

    def wait_window(n):
        sent = PLANE_ROWS - (ROWS if OFFSETS[n] == 0 else 0)
        wait_bytes(x_own.at[pl.ds(0, sent)], in_send.at[n])

    def send_next(first, last):
        for n in range(first, last):
            wait_window(n - LOOK)
            send_window(n)

    for n in range(LOOK):
        send_window(n)

    def new_momentum_step(k, carry):
        new_v[k] = momentum_of(k)
        return carry

    lax.fori_loop(0, MATS, new_momentum_step, 0)
    store_momentum = pltpu.make_async_copy(new_v, new_momentum_h, store_sem.at[0])
    store_momentum.start()

    wait_bytes(peak_y.at[pl.ds(0, experts - 1)], peak_recv.at[0])
    peak_z[z] = jnp.max(peak_y[...], axis=0)

    def send_peak_z(i, carry):
        remote(
            peak_z.at[z], peak_z.at[z], peak_send.at[1], peak_recv.at[1],
            {"dp": lax.rem(z + i, PLANES) * SEATS + seat},
        ).start()
        return carry

    lax.fori_loop(1, PLANES, send_peak_z, 0)

    def rows_of(i):
        return pl.ds(i * BLOCK, BLOCK)

    pair_copies = []
    far_copies = []
    share_copies = []

    def spot_of(s):
        first, count, columns = step_extent(s)
        rows, lanes = part_shape(s)
        if rows == count:
            return pl.ds(first, count), pl.ds(pl.multiple_of(core * lanes, LANES), lanes)
        return pl.ds(pl.multiple_of(first + core * rows, ROWS), rows), pl.ds(0, columns)

    def partial_gram(s):
        first, count, columns = step_extent(s)
        if part_shape(s)[0] == count:
            left, right = pl.ds(first, count), spot_of(s)[1]
        else:
            left, right = spot_of(s)[0], pl.ds(0, columns)
        return dot_nt(x_own[left, :], x_own[right, :]) + dot_nt(x_pair[left, :], x_pair[right, :])

    def share(s):
        far_copies[s].wait_recv()
        spot = spot_of(s)
        gram[spot] = (
            parts[s][...].astype(jnp.float32) + fars[s][...].astype(jnp.float32)
        ).astype(jnp.bfloat16)
        copy = remote(
            gram.at[spot], gram.at[spot], share_send.at[s], share_recv.at[s], {"dp": pair}
        )
        copy.start()
        share_copies.append(copy)

    def mirror(s):
        share_copies[s].wait_recv()
        first, count, _ = step_extent(s)
        if first:
            gram[0:first, first : first + count] = gram[first : first + count, 0:first].T

    def arrive(s):
        send_next(
            min(PLANES, STEP_SLOTS[s][0] + LOOK), min(PLANES, STEP_SLOTS[s][-1] + 1 + LOOK)
        )
        first, count, _ = step_extent(s)
        arrived = pl.ds(first, count)
        wait_bytes(x_own.at[arrived], in_recv.at[s])
        copy = remote(
            x_own.at[arrived], x_pair.at[arrived], pair_send.at[s], pair_recv.at[s], {"dp": pair}
        )
        copy.start()
        pair_copies.append(copy)

    arrive(0)
    for s in range(STEPS):
        if s + 1 < STEPS:
            arrive(s + 1)
        pair_copies[s].wait_recv()
        parts[s][...] = partial_gram(s).astype(jnp.bfloat16)
        copy = remote(parts[s], fars[s], far_send.at[s], far_recv.at[s], {"dp": across})
        copy.start()
        far_copies.append(copy)
        if s > 0:
            share(s - 1)
        if s > 1:
            mirror(s - 2)
    mirror(STEPS - 2)
    share(STEPS - 1)
    mirror(STEPS - 1)

    diagonal = gram[rows_of(0), rows_of(0)].astype(jnp.float32)
    for i in range(1, BLOCKS):
        diagonal = diagonal + gram[rows_of(i), rows_of(i)].astype(jnp.float32)
    down = lax.broadcasted_iota(jnp.int32, (BLOCK, BLOCK), 0)
    along = lax.broadcasted_iota(jnp.int32, (BLOCK, BLOCK), 1)
    squares = jnp.sum(jnp.where(down == along, diagonal, 0.0), axis=0, keepdims=True)
    squares = jnp.sum(squares, axis=1, keepdims=True)
    scale = lax.rsqrt(squares + EPSILON)
    scale2 = 1.0 / (squares + EPSILON)

    def half_rows(which, i):
        return pl.ds(pl.multiple_of(which * (HID // 2) + i * BLOCK, BLOCK), BLOCK)

    half_blocks = BLOCKS // 2
    poly_copies = []
    next_copies = []
    for i in range(half_blocks):
        rows = half_rows(core, i)
        poly[rows, :] = (
            (COEF_B * scale2) * gram[rows, :].astype(jnp.float32)
            + (COEF_C * scale2 * scale2) * dot_nn(gram[rows, :], gram[...])
        ).astype(jnp.bfloat16)
        copy = remote(
            poly.at[rows], poly.at[rows], poly_send.at[i], poly_recv.at[i], {"dp": pair}
        )
        copy.start()
        poly_copies.append(copy)

    def iterate_rows(rows):
        x_next[rows, :] = (
            scale
            * (COEF_A * x_own[rows, :].astype(jnp.float32) + dot_nn(poly[rows, :], x_own[...]))
        ).astype(jnp.bfloat16)

    for i in range(half_blocks):
        iterate_rows(half_rows(core, i))

    for i in range(half_blocks):
        rows = half_rows(core, i)
        left_v[i] = scale2 * (
            COEF_A * gram[rows, :].astype(jnp.float32) + dot_nn(poly[rows, :], gram[...])
        )
    for copy in poly_copies:
        copy.wait_recv()
    for i in range(half_blocks):
        rows = half_rows(core, i)
        left = left_v[i]
        gram_next[rows, :] = (
            COEF_A * left + dot_nn(left.astype(jnp.bfloat16), poly[...])
        ).astype(jnp.bfloat16)
        copy = remote(
            gram_next.at[rows], gram_next.at[rows], next_send.at[i], next_recv.at[i], {"dp": pair}
        )
        copy.start()
        next_copies.append(copy)
    for i in range(half_blocks):
        iterate_rows(half_rows(1 - core, i))

    wait_bytes(peak_z.at[pl.ds(0, PLANES - 1)], peak_recv.at[1])
    peak_s[seat] = jnp.max(peak_z[...], axis=0)

    def send_peak_s(i, carry):
        remote(
            peak_s.at[seat], peak_s.at[seat], peak_send.at[2], peak_recv.at[2],
            {"dp": z * SEATS + lax.rem(seat + i, SEATS)},
        ).start()
        return carry

    lax.fori_loop(1, SEATS, send_peak_s, 0)

    def send_update(slot):
        plane = wrapped(z + OFFSETS[slot])
        first = slot * PLANE_ROWS

        def send_rows(i, carry):
            their_seat = lax.rem(seat + i, SEATS)
            there = plane * SEATS + their_seat
            src = u_own.at[pl.ds(pl.multiple_of(first + their_seat * ROWS, ROWS), ROWS)]
            dst = returned_h.at[group, :, my_columns]

            @pl.when(there != me)
            def _():
                remote(src, dst, out_send, out_recv, {"dp": there}).start()

            @pl.when(there == me)
            def _():
                pltpu.make_async_copy(src, dst, out_recv).start()

            return carry

        lax.fori_loop(0, SEATS, send_rows, 0)
        spot = owned_h.at[0, 0, pl.ds(pl.multiple_of(plane * PLANE_ROWS, ROWS), PLANE_ROWS)]
        pltpu.make_async_copy(
            u_own.at[pl.ds(first, PLANE_ROWS)], spot, store_sem.at[1]
        ).start()

    for copy in next_copies:
        copy.wait_recv()
    for i in range(BLOCKS):
        rows = rows_of(i)
        own = gram_next[rows, :]
        term = (
            COEF_B * own.astype(jnp.float32) + COEF_C * dot_nn(own, gram_next[...])
        ).astype(jnp.bfloat16)
        last = (
            COEF_A * x_next[rows, :].astype(jnp.float32) + dot_nn(term, x_next[...])
        ).astype(jnp.bfloat16)
        u_own[rows, :] = (last.astype(jnp.float32) * math.sqrt(width)).astype(jnp.bfloat16)
        send_update(2 * i)
        send_update(2 * i + 1)

    for load in loads[4:]:
        load.wait()
    wait_bytes(peak_s.at[pl.ds(0, SEATS - 1)], peak_recv.at[2])
    top = jnp.max(peak_s[...], axis=0)
    head_down = lax.broadcasted_iota(jnp.int32, (HEADS, HEADS), 0)
    head_along = lax.broadcasted_iota(jnp.int32, (HEADS, HEADS), 1)
    same = head_down == head_along
    peak = jnp.max(
        jnp.where(same, jnp.broadcast_to(top[0:1, 0:HEADS], (HEADS, HEADS)), 0.0),
        axis=1, keepdims=True,
    )
    flag = jnp.max(
        jnp.where(
            same, jnp.broadcast_to(flags_v[...].astype(jnp.float32), (HEADS, HEADS)), 0.0
        ),
        axis=1, keepdims=True,
    )
    peak = jnp.broadcast_to(peak, (HEADS, LANES))
    flag = jnp.broadcast_to(flag, (HEADS, LANES))
    gamma = jnp.where(flag == 1.0, jnp.minimum(1.0, CLIP_TAU / peak), 1.0)
    gamma_v[...] = gamma
    root_v[...] = jnp.sqrt(gamma)
    low = lax.broadcasted_iota(jnp.int32, (1, LANES), 1) < LANES // 2

    def clip_step(j, carry):
        root0 = root_v[pl.ds(2 * j, 1), :]
        root1 = root_v[pl.ds(2 * j + 1, 1), :]
        gamma0 = gamma_v[pl.ds(2 * j, 1), :]
        gamma1 = gamma_v[pl.ds(2 * j + 1, 1), :]
        scales = (root0, jnp.where(low, gamma0, root1), jnp.where(low, root1, gamma1))
        for n, factor in enumerate(scales):
            lanes = pl.ds(pl.multiple_of((3 * j + n) * LANES, LANES), LANES)
            query_o[:, lanes] = (query_v[:, lanes].astype(jnp.float32) * factor).astype(
                jnp.bfloat16
            )
        for n, factor in enumerate((root0, root1)):
            lanes = pl.ds(pl.multiple_of((2 * j + n) * LANES, LANES), LANES)
            key_o[:, lanes] = (key_v[:, lanes].astype(jnp.float32) * factor).astype(jnp.bfloat16)
        return carry

    lax.fori_loop(0, HEADS // 2, clip_step, 0)
    store_query = pltpu.make_async_copy(query_o, query_out_h, store_sem.at[2])
    store_key = pltpu.make_async_copy(key_o, key_out_h, store_sem.at[3])
    store_query.start()
    store_key.start()

    store_momentum.wait()
    store_query.wait()
    store_key.wait()
    wait_bytes(peak_y.at[pl.ds(0, experts - 1)], peak_send.at[0])
    wait_bytes(peak_z.at[pl.ds(0, PLANES - 1)], peak_send.at[1])
    wait_bytes(peak_s.at[pl.ds(0, SEATS - 1)], peak_send.at[2])
    for copy in pair_copies + far_copies + share_copies + poly_copies + next_copies:
        copy.wait_send()
    for n in range(PLANES - LOOK, PLANES):
        wait_window(n)
    wait_bytes(u_own.at[pl.ds(0, HID - ROWS)], out_send)
    wait_bytes(u_own, store_sem.at[1])

    wait_bytes(returned_h, out_recv)


def finish_kernel(
    owner_h, new_momentum_i, returned_i, owned_i, query_i, key_i,
    new_momentum_h, update_h, owned_h, query_h, key_h,
    owner_s, new_momentum_v, returned_v, owned_v, query_v, key_v,
    owner_sem, load_sem, store_sem, pick_sem, put_sem,
):
    load_owner = pltpu.make_async_copy(owner_h, owner_s, owner_sem)
    load_owner.start()
    plain = (
        (new_momentum_i, new_momentum_v, new_momentum_h),
        (owned_i, owned_v, owned_h),
        (query_i, query_v, query_h),
        (key_i, key_v, key_h),
    )
    loads = [
        pltpu.make_async_copy(src, mid, load_sem.at[n]) for n, (src, mid, _) in enumerate(plain)
    ]
    stores = [
        pltpu.make_async_copy(mid, dst, store_sem.at[n]) for n, (_, mid, dst) in enumerate(plain)
    ]
    for load in loads:
        load.start()
    load_returned = pltpu.make_async_copy(returned_i, returned_v, pick_sem)
    load_returned.start()
    for load, store in zip(loads, stores):
        load.wait()
        store.start()
    load_owner.wait()
    load_returned.wait()
    puts = [
        pltpu.make_async_copy(returned_v.at[owner_s[0, k]], update_h.at[k], put_sem.at[k])
        for k in range(MATS)
    ]
    for put in puts:
        put.start()
    for copy in stores + puts:
        copy.wait()


def shards(experts, grads, momentum, owner, query_weight, key_weight, head_maxima, clip_flags):
    mats, rows, width = grads.shape
    quarter = width // 4
    anywhere = pl.BlockSpec(memory_space=pl.ANY)
    bf16 = jnp.bfloat16
    shard = jax.ShapeDtypeStruct((mats, rows, width), bf16)
    block = pltpu.VMEM((mats, rows, width), bf16)
    half = pltpu.VMEM((HID, quarter), bf16)
    square = pltpu.VMEM((HID, HID), bf16)
    lanes = [pltpu.VMEM(part_shape(s), bf16) for s in range(STEPS)]
    dma = pltpu.SemaphoreType.DMA
    results = (
        shard,
        shard,
        jax.ShapeDtypeStruct((1, 1, HID, quarter), bf16),
        jax.ShapeDtypeStruct(query_weight.shape, bf16),
        jax.ShapeDtypeStruct(key_weight.shape, bf16),
    )
    parts = pl.pallas_call(
        functools.partial(step_kernel, experts),
        out_shape=results,
        in_specs=[anywhere] * 7,
        out_specs=(anywhere,) * 5,
        scratch_shapes=[
            pltpu.SMEM((1, mats), jnp.int32),
            pltpu.VMEM((1, HEADS), jnp.float32),
            pltpu.VMEM((1, HEADS), jnp.int32),
            pltpu.VMEM(query_weight.shape, bf16),
            pltpu.VMEM(key_weight.shape, bf16),
            pltpu.VMEM(query_weight.shape, bf16),
            pltpu.VMEM(key_weight.shape, bf16),
            block, block, block, block, half, half, half, half, square, square, square,
            pltpu.VMEM((BLOCKS // 2, BLOCK, HID), jnp.float32),
            *lanes, *lanes,
            pltpu.VMEM((experts, 8, LANES), jnp.float32),
            pltpu.VMEM((PLANES, 8, LANES), jnp.float32),
            pltpu.VMEM((SEATS, 8, LANES), jnp.float32),
            pltpu.VMEM((HEADS, LANES), jnp.float32),
            pltpu.VMEM((HEADS, LANES), jnp.float32),
            dma((7,)), dma((4,)), dma((PLANES,)), dma((STEPS,)), dma((STEPS,)), dma((STEPS,)),
            dma((STEPS,)), dma((STEPS,)), dma((STEPS,)), dma((STEPS,)),
            *[dma((BLOCKS // 2,))] * 4, dma, dma,
            dma((3,)), dma((3,)),
        ],
        compiler_params=pltpu.CompilerParams(
            collective_id=0, has_side_effects=True, vmem_limit_bytes=60 * 1024 * 1024
        ),
        name="muon_step",
    )(
        owner, grads, momentum, query_weight, key_weight, head_maxima,
        clip_flags.reshape(1, HEADS),
    )
    return pl.pallas_call(
        finish_kernel,
        out_shape=results,
        in_specs=[anywhere] * 6,
        out_specs=(anywhere,) * 5,
        scratch_shapes=[
            pltpu.SMEM((1, mats), jnp.int32),
            *[pltpu.VMEM(result.shape, bf16) for result in results],
            dma, dma((4,)), dma((4,)), dma, dma((MATS,)),
        ],
        compiler_params=pltpu.CompilerParams(vmem_limit_bytes=60 * 1024 * 1024),
        name="finish",
    )(owner, *parts)


def solution(mesh):
    in_specs = (
        P("expert", "dp", None),
        P("expert", "dp", None),
        P("expert", None),
        P("dp", None),
        P("dp", None),
        P(("dp", "expert"), None),
        P(),
    )
    out_specs = (
        P("expert", "dp", None),
        P("expert", "dp", None),
        P("expert", "dp", None, None),
        P("dp", None),
        P("dp", None),
    )
    return jax.shard_map(
        functools.partial(shards, mesh.shape["expert"]),
        mesh=mesh, in_specs=in_specs, out_specs=out_specs, check_vma=False,
    )
```

```python
import functools
import math

import jax
import jax.numpy as jnp
from jax import lax
from jax.experimental import pallas as pl
from jax.experimental.pallas import tpu as pltpu
from jax.sharding import PartitionSpec as P

HEADS = 64
QNOPE = 128
QROPE = 64

MOMENTUM_DECAY = 0.95
COEF_A = 3.4445
COEF_B = -4.775
COEF_C = 2.0315
EPSILON = 1e-07
CLIP_TAU = 100.0

MESH = pl.DeviceIdType.MESH
PLANES = 8
SEATS = 8
ROWS = 16
MATS = 16
PLANE_ROWS = SEATS * ROWS
BLOCK = 2 * PLANE_ROWS
HID = PLANES * PLANE_ROWS
DEVICES = PLANES * SEATS
LANES = 128

OFFSETS = (3, -3, 2, -2, 1, -1, 0, 4)
LOOK = 8
LAG = 3
STEP_SLOTS = tuple((n,) for n in range(PLANES))
STEPS = len(STEP_SLOTS)
BLOCKS = HID // BLOCK


def wrapped(value):
    return lax.rem(value + 64, 8)


def step_extent(s):
    first = STEP_SLOTS[s][0] * PLANE_ROWS
    count = len(STEP_SLOTS[s]) * PLANE_ROWS
    return first, count, first + count


def part_shape(s):
    _, count, columns = step_extent(s)
    return (count, columns // 2) if columns % BLOCK == 0 and count == BLOCK else (count // 2, columns)


def dot_nn(a, b):
    return jnp.dot(a, b, preferred_element_type=jnp.float32)


def dot_nt(a, b):
    return lax.dot_general(a, b, (((1,), (1,)), ((), ())), preferred_element_type=jnp.float32)


def wait_bytes(ref, sem):
    pltpu.make_async_copy(ref, ref, sem).wait()


def step_kernel(
    experts,
    owner_h, grads_h, momentum_h, query_h, key_h, peaks_h, flags_h,
    new_momentum_h, returned_h, owned_h, query_out_h, key_out_h,
    owner_s, peaks_v, flags_v, query_v, key_v, query_o, key_o,
    grads_v, momentum_v, staged, new_v, x_own, x_pair, x_next, u_own,
    gram, poly, gram_next, left_v,
    part0, part1, part2, part3, part4, part5, part6, part7,
    far0, far1, far2, far3, far4, far5, far6, far7,
    peak_y, peak_z, peak_s, gamma_v, root_v,
    load_sem, store_sem, in_send, in_recv, pair_send, pair_recv,
    far_send, far_recv, share_send, share_recv, poly_send, poly_recv, next_send, next_recv,
    out_send, out_recv,
    peak_send, peak_recv,
):
    parts = (part0, part1, part2, part3, part4, part5, part6, part7)
    fars = (far0, far1, far2, far3, far4, far5, far6, far7)
    me = lax.axis_index("dp")
    y = lax.axis_index("expert")
    z = me // SEATS
    seat = lax.rem(me, SEATS)
    core = lax.rem(me, 2)
    group = me // 4
    width = grads_v.shape[2]
    quarter = width // 4
    pair = me + 1 - 2 * core
    across = me + 2 - 4 * lax.rem(me // 2, 2)

    def columns_of(part):
        return pl.ds(pl.multiple_of(part * quarter, LANES), quarter)

    my_columns = columns_of(lax.rem(me, 4))

    def remote(src, dst, send, recv, where):
        return pltpu.make_async_remote_copy(
            src_ref=src, dst_ref=dst, send_sem=send, recv_sem=recv,
            device_id=where, device_id_type=MESH,
        )

    loads = [
        pltpu.make_async_copy(src, dst, load_sem.at[n])
        for n, (src, dst) in enumerate(
            (
                (owner_h, owner_s),
                (grads_h, grads_v),
                (momentum_h, momentum_v),
                (peaks_h, peaks_v),
                (flags_h, flags_v),
                (query_h, query_v),
                (key_h, key_v),
            )
        )
    ]
    for load in loads:
        load.start()

    barrier = pltpu.get_barrier_semaphore()

    def greet(i, carry):
        pl.semaphore_signal(
            barrier, inc=1, device_id={"dp": lax.rem(me + i, DEVICES)}, device_id_type=MESH
        )
        return carry

    lax.fori_loop(1, DEVICES, greet, 0)

    def greet_expert(i, carry):
        pl.semaphore_signal(
            barrier, inc=1, device_id={"expert": lax.rem(y + i, experts)}, device_id_type=MESH
        )
        return carry

    lax.fori_loop(1, experts, greet_expert, 0)

    for load in loads[:4]:
        load.wait()
    peak_y[y] = jnp.zeros((8, LANES), jnp.float32)
    peak_y[y, :, 0:HEADS] = jnp.broadcast_to(peaks_v[...], (8, HEADS))

    def momentum_of(k):
        return (
            MOMENTUM_DECAY * momentum_v[k].astype(jnp.float32) + grads_v[k].astype(jnp.float32)
        ).astype(jnp.bfloat16)

    def stage(g, carry):
        k = jnp.int32(0)
        for m in range(MATS):
            k = jnp.where(owner_s[0, m] == g, m, k)
        staged[g] = momentum_of(k)
        return carry

    pl.semaphore_wait(barrier, DEVICES - 1 + experts - 1)

    def send_peak_y(i, carry):
        remote(
            peak_y.at[y], peak_y.at[y], peak_send.at[0], peak_recv.at[0],
            {"expert": lax.rem(y + i, experts)},
        ).start()
        return carry

    lax.fori_loop(1, experts, send_peak_y, 0)

    def send_window(n):
        their_z = wrapped(z - OFFSETS[n])
        lax.fori_loop(2 * their_z, 2 * their_z + 2, stage, 0)
        dst = x_own.at[pl.ds(pl.multiple_of(n * PLANE_ROWS + seat * ROWS, ROWS), ROWS)]
        arrival = in_recv.at[[n in slots for slots in STEP_SLOTS].index(True)]

        def send_rows(i, carry):
            there = their_z * SEATS + lax.rem(seat + i, SEATS)
            src = staged.at[there // 4, :, columns_of(lax.rem(there, 4))]

            @pl.when(there != me)
            def _():
                remote(src, dst, in_send.at[n], arrival, {"dp": there}).start()

            @pl.when(there == me)
            def _():
                pltpu.make_async_copy(src, dst, arrival).start()

            return carry

        lax.fori_loop(0, SEATS, send_rows, 0)

    def wait_window(n):
        sent = PLANE_ROWS - (ROWS if OFFSETS[n] == 0 else 0)
        wait_bytes(x_own.at[pl.ds(0, sent)], in_send.at[n])

    def send_next(first, last):
        for n in range(first, last):
            wait_window(n - LOOK)
            send_window(n)

    for n in range(LOOK):
        send_window(n)

    def new_momentum_step(k, carry):
        new_v[k] = momentum_of(k)
        return carry

    lax.fori_loop(0, MATS, new_momentum_step, 0)
    store_momentum = pltpu.make_async_copy(new_v, new_momentum_h, store_sem.at[0])
    store_momentum.start()

    wait_bytes(peak_y.at[pl.ds(0, experts - 1)], peak_recv.at[0])
    peak_z[z] = jnp.max(peak_y[...], axis=0)

    def send_peak_z(i, carry):
        remote(
            peak_z.at[z], peak_z.at[z], peak_send.at[1], peak_recv.at[1],
            {"dp": lax.rem(z + i, PLANES) * SEATS + seat},
        ).start()
        return carry

    lax.fori_loop(1, PLANES, send_peak_z, 0)

    def rows_of(i):
        return pl.ds(i * BLOCK, BLOCK)

    pair_copies = []
    far_copies = []
    share_copies = []

    def spot_of(s):
        first, count, columns = step_extent(s)
        rows, lanes = part_shape(s)
        if rows == count:
            return pl.ds(first, count), pl.ds(pl.multiple_of(core * lanes, LANES), lanes)
        return pl.ds(pl.multiple_of(first + core * rows, ROWS), rows), pl.ds(0, columns)

    def partial_gram(s):
        first, count, columns = step_extent(s)
        if part_shape(s)[0] == count:
            left, right = pl.ds(first, count), spot_of(s)[1]
        else:
            left, right = spot_of(s)[0], pl.ds(0, columns)
        return dot_nt(x_own[left, :], x_own[right, :]) + dot_nt(x_pair[left, :], x_pair[right, :])

    def share(s):
        far_copies[s].wait_recv()
        spot = spot_of(s)
        gram[spot] = (
            parts[s][...].astype(jnp.float32) + fars[s][...].astype(jnp.float32)
        ).astype(jnp.bfloat16)
        copy = remote(
            gram.at[spot], gram.at[spot], share_send.at[s], share_recv.at[s], {"dp": pair}
        )
        copy.start()
        share_copies.append(copy)

    def mirror(s):
        share_copies[s].wait_recv()
        first, count, _ = step_extent(s)
        if first:
            gram[0:first, first : first + count] = gram[first : first + count, 0:first].T

    def arrive(s):
        send_next(
            min(PLANES, STEP_SLOTS[s][0] + LOOK), min(PLANES, STEP_SLOTS[s][-1] + 1 + LOOK)
        )
        first, count, _ = step_extent(s)
        arrived = pl.ds(first, count)
        wait_bytes(x_own.at[arrived], in_recv.at[s])
        copy = remote(
            x_own.at[arrived], x_pair.at[arrived], pair_send.at[s], pair_recv.at[s], {"dp": pair}
        )
        copy.start()
        pair_copies.append(copy)

    arrive(0)
    for s in range(STEPS):
        if s + 1 < STEPS:
            arrive(s + 1)
        pair_copies[s].wait_recv()
        parts[s][...] = partial_gram(s).astype(jnp.bfloat16)
        copy = remote(parts[s], fars[s], far_send.at[s], far_recv.at[s], {"dp": across})
        copy.start()
        far_copies.append(copy)
        if s >= LAG:
            share(s - LAG)
        if s > LAG:
            mirror(s - LAG - 1)
    for s in range(STEPS - LAG, STEPS):
        share(s)
        mirror(s - 1)
    mirror(STEPS - 1)

    diagonal = gram[rows_of(0), rows_of(0)].astype(jnp.float32)
    for i in range(1, BLOCKS):
        diagonal = diagonal + gram[rows_of(i), rows_of(i)].astype(jnp.float32)
    down = lax.broadcasted_iota(jnp.int32, (BLOCK, BLOCK), 0)
    along = lax.broadcasted_iota(jnp.int32, (BLOCK, BLOCK), 1)
    squares = jnp.sum(jnp.where(down == along, diagonal, 0.0), axis=0, keepdims=True)
    squares = jnp.sum(squares, axis=1, keepdims=True)
    scale = lax.rsqrt(squares + EPSILON)
    scale2 = 1.0 / (squares + EPSILON)

    def half_rows(which, i):
        return pl.ds(pl.multiple_of(which * (HID // 2) + i * BLOCK, BLOCK), BLOCK)

    half_blocks = BLOCKS // 2
    poly_copies = []
    next_copies = []
    for i in range(half_blocks):
        rows = half_rows(core, i)
        poly[rows, :] = (
            (COEF_B * scale2) * gram[rows, :].astype(jnp.float32)
            + (COEF_C * scale2 * scale2) * dot_nn(gram[rows, :], gram[...])
        ).astype(jnp.bfloat16)
        copy = remote(
            poly.at[rows], poly.at[rows], poly_send.at[i], poly_recv.at[i], {"dp": pair}
        )
        copy.start()
        poly_copies.append(copy)

    def iterate_rows(rows):
        x_next[rows, :] = (
            scale
            * (COEF_A * x_own[rows, :].astype(jnp.float32) + dot_nn(poly[rows, :], x_own[...]))
        ).astype(jnp.bfloat16)

    for i in range(half_blocks):
        iterate_rows(half_rows(core, i))

    for i in range(half_blocks):
        rows = half_rows(core, i)
        left_v[i] = scale2 * (
            COEF_A * gram[rows, :].astype(jnp.float32) + dot_nn(poly[rows, :], gram[...])
        )
    for copy in poly_copies:
        copy.wait_recv()
    for i in range(half_blocks):
        rows = half_rows(core, i)
        left = left_v[i]
        gram_next[rows, :] = (
            COEF_A * left + dot_nn(left.astype(jnp.bfloat16), poly[...])
        ).astype(jnp.bfloat16)
        copy = remote(
            gram_next.at[rows], gram_next.at[rows], next_send.at[i], next_recv.at[i], {"dp": pair}
        )
        copy.start()
        next_copies.append(copy)
    for i in range(half_blocks):
        iterate_rows(half_rows(1 - core, i))

    wait_bytes(peak_z.at[pl.ds(0, PLANES - 1)], peak_recv.at[1])
    peak_s[seat] = jnp.max(peak_z[...], axis=0)

    def send_peak_s(i, carry):
        remote(
            peak_s.at[seat], peak_s.at[seat], peak_send.at[2], peak_recv.at[2],
            {"dp": z * SEATS + lax.rem(seat + i, SEATS)},
        ).start()
        return carry

    lax.fori_loop(1, SEATS, send_peak_s, 0)

    def send_update(slot):
        plane = wrapped(z + OFFSETS[slot])
        first = slot * PLANE_ROWS

        def send_rows(i, carry):
            their_seat = lax.rem(seat + i, SEATS)
            there = plane * SEATS + their_seat
            src = u_own.at[pl.ds(pl.multiple_of(first + their_seat * ROWS, ROWS), ROWS)]
            dst = returned_h.at[group, :, my_columns]

            @pl.when(there != me)
            def _():
                remote(src, dst, out_send, out_recv, {"dp": there}).start()

            @pl.when(there == me)
            def _():
                pltpu.make_async_copy(src, dst, out_recv).start()

            return carry

        lax.fori_loop(0, SEATS, send_rows, 0)
        spot = owned_h.at[0, 0, pl.ds(pl.multiple_of(plane * PLANE_ROWS, ROWS), PLANE_ROWS)]
        pltpu.make_async_copy(
            u_own.at[pl.ds(first, PLANE_ROWS)], spot, store_sem.at[1]
        ).start()

    for copy in next_copies:
        copy.wait_recv()
    for slots in ((0,), (1,), (2, 3), (4, 5), (6, 7)):
        rows = pl.ds(slots[0] * PLANE_ROWS, len(slots) * PLANE_ROWS)
        own = gram_next[rows, :]
        term = (
            COEF_B * own.astype(jnp.float32) + COEF_C * dot_nn(own, gram_next[...])
        ).astype(jnp.bfloat16)
        last = (
            COEF_A * x_next[rows, :].astype(jnp.float32) + dot_nn(term, x_next[...])
        ).astype(jnp.bfloat16)
        u_own[rows, :] = (last.astype(jnp.float32) * math.sqrt(width)).astype(jnp.bfloat16)
        for slot in slots:
            send_update(slot)

    for load in loads[4:]:
        load.wait()
    wait_bytes(peak_s.at[pl.ds(0, SEATS - 1)], peak_recv.at[2])
    top = jnp.max(peak_s[...], axis=0)
    head_down = lax.broadcasted_iota(jnp.int32, (HEADS, HEADS), 0)
    head_along = lax.broadcasted_iota(jnp.int32, (HEADS, HEADS), 1)
    same = head_down == head_along
    peak = jnp.max(
        jnp.where(same, jnp.broadcast_to(top[0:1, 0:HEADS], (HEADS, HEADS)), 0.0),
        axis=1, keepdims=True,
    )
    flag = jnp.max(
        jnp.where(
            same, jnp.broadcast_to(flags_v[...].astype(jnp.float32), (HEADS, HEADS)), 0.0
        ),
        axis=1, keepdims=True,
    )
    peak = jnp.broadcast_to(peak, (HEADS, LANES))
    flag = jnp.broadcast_to(flag, (HEADS, LANES))
    gamma = jnp.where(flag == 1.0, jnp.minimum(1.0, CLIP_TAU / peak), 1.0)
    gamma_v[...] = gamma
    root_v[...] = jnp.sqrt(gamma)
    low = lax.broadcasted_iota(jnp.int32, (1, LANES), 1) < LANES // 2

    def clip_step(j, carry):
        root0 = root_v[pl.ds(2 * j, 1), :]
        root1 = root_v[pl.ds(2 * j + 1, 1), :]
        gamma0 = gamma_v[pl.ds(2 * j, 1), :]
        gamma1 = gamma_v[pl.ds(2 * j + 1, 1), :]
        scales = (root0, jnp.where(low, gamma0, root1), jnp.where(low, root1, gamma1))
        for n, factor in enumerate(scales):
            lanes = pl.ds(pl.multiple_of((3 * j + n) * LANES, LANES), LANES)
            query_o[:, lanes] = (query_v[:, lanes].astype(jnp.float32) * factor).astype(
                jnp.bfloat16
            )
        for n, factor in enumerate((root0, root1)):
            lanes = pl.ds(pl.multiple_of((2 * j + n) * LANES, LANES), LANES)
            key_o[:, lanes] = (key_v[:, lanes].astype(jnp.float32) * factor).astype(jnp.bfloat16)
        return carry

    lax.fori_loop(0, HEADS // 2, clip_step, 0)
    store_query = pltpu.make_async_copy(query_o, query_out_h, store_sem.at[2])
    store_key = pltpu.make_async_copy(key_o, key_out_h, store_sem.at[3])
    store_query.start()
    store_key.start()

    store_momentum.wait()
    store_query.wait()
    store_key.wait()
    wait_bytes(peak_y.at[pl.ds(0, experts - 1)], peak_send.at[0])
    wait_bytes(peak_z.at[pl.ds(0, PLANES - 1)], peak_send.at[1])
    wait_bytes(peak_s.at[pl.ds(0, SEATS - 1)], peak_send.at[2])
    for copy in pair_copies + far_copies + share_copies + poly_copies + next_copies:
        copy.wait_send()
    for n in range(PLANES - LOOK, PLANES):
        wait_window(n)
    wait_bytes(u_own.at[pl.ds(0, HID - ROWS)], out_send)
    wait_bytes(u_own, store_sem.at[1])

    wait_bytes(returned_h, out_recv)


def finish_kernel(
    owner_h, new_momentum_i, returned_i, owned_i, query_i, key_i,
    new_momentum_h, update_h, owned_h, query_h, key_h,
    owner_s, new_momentum_v, returned_v, owned_v, query_v, key_v,
    owner_sem, load_sem, store_sem, pick_sem, put_sem,
):
    load_owner = pltpu.make_async_copy(owner_h, owner_s, owner_sem)
    load_owner.start()
    plain = (
        (new_momentum_i, new_momentum_v, new_momentum_h),
        (owned_i, owned_v, owned_h),
        (query_i, query_v, query_h),
        (key_i, key_v, key_h),
    )
    loads = [
        pltpu.make_async_copy(src, mid, load_sem.at[n]) for n, (src, mid, _) in enumerate(plain)
    ]
    stores = [
        pltpu.make_async_copy(mid, dst, store_sem.at[n]) for n, (_, mid, dst) in enumerate(plain)
    ]
    for load in loads:
        load.start()
    load_returned = pltpu.make_async_copy(returned_i, returned_v, pick_sem)
    load_returned.start()
    for load, store in zip(loads, stores):
        load.wait()
        store.start()
    load_owner.wait()
    load_returned.wait()
    puts = [
        pltpu.make_async_copy(returned_v.at[owner_s[0, k]], update_h.at[k], put_sem.at[k])
        for k in range(MATS)
    ]
    for put in puts:
        put.start()
    for copy in stores + puts:
        copy.wait()


def shards(experts, grads, momentum, owner, query_weight, key_weight, head_maxima, clip_flags):
    mats, rows, width = grads.shape
    quarter = width // 4
    anywhere = pl.BlockSpec(memory_space=pl.ANY)
    bf16 = jnp.bfloat16
    shard = jax.ShapeDtypeStruct((mats, rows, width), bf16)
    block = pltpu.VMEM((mats, rows, width), bf16)
    half = pltpu.VMEM((HID, quarter), bf16)
    square = pltpu.VMEM((HID, HID), bf16)
    lanes = [pltpu.VMEM(part_shape(s), bf16) for s in range(STEPS)]
    dma = pltpu.SemaphoreType.DMA
    results = (
        shard,
        shard,
        jax.ShapeDtypeStruct((1, 1, HID, quarter), bf16),
        jax.ShapeDtypeStruct(query_weight.shape, bf16),
        jax.ShapeDtypeStruct(key_weight.shape, bf16),
    )
    parts = pl.pallas_call(
        functools.partial(step_kernel, experts),
        out_shape=results,
        in_specs=[anywhere] * 7,
        out_specs=(anywhere,) * 5,
        scratch_shapes=[
            pltpu.SMEM((1, mats), jnp.int32),
            pltpu.VMEM((1, HEADS), jnp.float32),
            pltpu.VMEM((1, HEADS), jnp.int32),
            pltpu.VMEM(query_weight.shape, bf16),
            pltpu.VMEM(key_weight.shape, bf16),
            pltpu.VMEM(query_weight.shape, bf16),
            pltpu.VMEM(key_weight.shape, bf16),
            block, block, block, block, half, half, half, half, square, square, square,
            pltpu.VMEM((BLOCKS // 2, BLOCK, HID), jnp.float32),
            *lanes, *lanes,
            pltpu.VMEM((experts, 8, LANES), jnp.float32),
            pltpu.VMEM((PLANES, 8, LANES), jnp.float32),
            pltpu.VMEM((SEATS, 8, LANES), jnp.float32),
            pltpu.VMEM((HEADS, LANES), jnp.float32),
            pltpu.VMEM((HEADS, LANES), jnp.float32),
            dma((7,)), dma((4,)), dma((PLANES,)), dma((STEPS,)), dma((STEPS,)), dma((STEPS,)),
            dma((STEPS,)), dma((STEPS,)), dma((STEPS,)), dma((STEPS,)),
            *[dma((BLOCKS // 2,))] * 4, dma, dma,
            dma((3,)), dma((3,)),
        ],
        compiler_params=pltpu.CompilerParams(
            collective_id=0, has_side_effects=True, vmem_limit_bytes=60 * 1024 * 1024
        ),
        name="muon_step",
    )(
        owner, grads, momentum, query_weight, key_weight, head_maxima,
        clip_flags.reshape(1, HEADS),
    )
    return pl.pallas_call(
        finish_kernel,
        out_shape=results,
        in_specs=[anywhere] * 6,
        out_specs=(anywhere,) * 5,
        scratch_shapes=[
            pltpu.SMEM((1, mats), jnp.int32),
            *[pltpu.VMEM(result.shape, bf16) for result in results],
            dma, dma((4,)), dma((4,)), dma, dma((MATS,)),
        ],
        compiler_params=pltpu.CompilerParams(vmem_limit_bytes=60 * 1024 * 1024),
        name="finish",
    )(owner, *parts)


def solution(mesh):
    in_specs = (
        P("expert", "dp", None),
        P("expert", "dp", None),
        P("expert", None),
        P("dp", None),
        P("dp", None),
        P(("dp", "expert"), None),
        P(),
    )
    out_specs = (
        P("expert", "dp", None),
        P("expert", "dp", None),
        P("expert", "dp", None, None),
        P("dp", None),
        P("dp", None),
    )
    return jax.shard_map(
        functools.partial(shards, mesh.shape["expert"]),
        mesh=mesh, in_specs=in_specs, out_specs=out_specs, check_vma=False,
    )
```
